32 devices in a mesh: groups: 2 (over x), batch: 8 (over z, y), tensor: 2 (over core).
Axes of the slice: x: 2, y: 2, z: 4, core: 2. Of those that a mesh axis runs over, the one named last changes fastest.
Arguments:
- teacher_rows: bfloat16 [8192, 6144], P(('groups', 'batch'), 'tensor'), parts along dimension 0, may hold values from -6 to 6
- teacher_gain: bfloat16 [6144], P('tensor'), may hold values from 0.099609375 to 1.8984375
- head_weight: bfloat16 [6144, 1024], P('tensor'), may hold values from -0.078125 to 0.078125
- student_slot: int32 [8192], P(('groups', 'batch')), parts along dimension 0, may hold values from 0 to 4095, as said below
- student_rows: bfloat16 [8192, 1024], P(('groups', 'batch')), parts along dimension 0, may hold values from -6 to 6
- student_gain: bfloat16 [1024], replicated, may hold values from 0.099609375 to 1.8984375
- up_weight: bfloat16 [1024, 2048], P(None, 'tensor'), may hold values from -0.1875 to 0.1875
- down_weight: bfloat16 [2048, 1024], P('tensor'), may hold values from -0.125 to 0.125
Outputs:
- grad_up: float32 [2048, 2048], P(('groups', 'batch'), 'tensor'), parts along dimension 0
- grad_down: float32 [4096, 1024], P(('groups', 'tensor'), 'batch'), parts along dimension 0
The draws below stay inside these ranges and needn't reach their ends.
There are 2 independent parts, one for each index of `groups`. The reference program is written for one: setup_inputs(seed, part) draws one part's arguments, and reference() takes and returns one part's arrays. A program takes and returns all parts, laid end to end along the dimension named above; an argument that names none is the same for every part. Nothing has to cross between parts.
Inputs may be any that keep to these rules, and one draw needn't show every extreme that they name: `student_slot`: A permutation of the 4096 rows. The rows of one index of batch send at most 128 rows into any one block of 512 rows of the student order, and exactly 128 into some.
All inputs are finite; a program needn't handle non-finite values.
Results may differ from the reference program's by a relative error of at most 0.0044.
Values may be sent and summed in bfloat16 or wider, within the bound.
A program may use at most 128 MiB of HBM per device.

```python
import jax
import jax.numpy as jnp
from jax import lax

DT = 6144
DS = 1024
HS = 2048
TOK_DEV = 512
TOKENS = 4096


def draw_student_slot(key, part):
    key = jax.random.fold_in(key, 11)
    peers = TOKENS // TOK_DEV
    unit = TOK_DEV // peers
    key_shift, key_place, key_rows = jax.random.split(key, 3)
    order = jax.random.permutation(key_shift, peers)
    weight = jnp.where(order < peers // 4, 2 * unit, jnp.where(order < 3 * peers // 4, unit, 0)).astype(jnp.int32)
    ends = jnp.cumsum(weight)
    index = jnp.arange(TOK_DEV, dtype=jnp.int32)
    shift = jnp.sum((ends[None, :] <= index[:, None]).astype(jnp.int32), axis=1)
    source = jnp.arange(peers, dtype=jnp.int32)
    dest = (source[:, None] + shift[None, :]) % peers
    place = jax.vmap(lambda one: jax.random.permutation(one, TOK_DEV))(jax.random.split(key_place, peers)).astype(jnp.int32)
    ordered = dest * TOK_DEV + place[dest, index[None, :]]
    row_order = jax.vmap(lambda one: jax.random.permutation(one, TOK_DEV))(jax.random.split(key_rows, peers)).astype(jnp.int32)
    slots = jnp.take_along_axis(ordered, row_order, axis=1)
    return slots.reshape(-1).astype(jnp.int32)


def levels(own_key, extent, pieces, smallest, high):
    level = 1.0
    for axis_at, blocks in pieces:
        draws = jax.random.uniform(jax.random.fold_in(jax.random.fold_in(own_key, 6), axis_at), (blocks,), jnp.float32, smallest / len(pieces), high / len(pieces))
        level = level * jnp.repeat(jnp.exp(draws), extent[axis_at] // blocks).reshape((-1,) + (1,) * (len(extent) - 1 - axis_at))
    return level


def centred(key, extent, spread, bound, cuts=(), kind=jnp.bfloat16):
    array = spread * jax.random.normal(key, extent, jnp.float32)
    if cuts:
        array = array * levels(key, extent, cuts, -0.22, 0.18)
    return jnp.clip(array, -bound, bound).astype(kind)


def setup_inputs(seed: int = 0, part: int = 0) -> dict:
    streams_of = jax.random.split(jax.random.key(seed), 9)
    own_keys = jax.random.split(jax.random.fold_in(streams_of[8], part), 9)
    return {
        "teacher_rows": centred(own_keys[0], (TOKENS, DT), 1.0, 6.0, ((0, 8), (1, 2))),
        "teacher_gain": jnp.clip(1.0 + 0.18 * jax.random.normal(streams_of[1], (DT,), jnp.float32), 0.099609375, 1.8984375).astype(jnp.bfloat16),
        "head_weight": centred(streams_of[2], (DT, DS), DT ** -0.5, 0.078125, ((0, 2),)),
        "student_slot": draw_student_slot(jax.random.fold_in(jax.random.fold_in(streams_of[8], part), 71), part),
        "student_rows": centred(own_keys[4], (TOKENS, DS), 1.0, 6.0, ((0, 8),)),
        "student_gain": jnp.clip(1.0 + 0.18 * jax.random.normal(streams_of[5], (DS,), jnp.float32), 0.099609375, 1.8984375).astype(jnp.bfloat16),
        "up_weight": centred(streams_of[6], (DS, HS), DS ** -0.5, 0.1875, ((1, 2),)),
        "down_weight": centred(streams_of[7], (HS, DS), HS ** -0.5, 0.125, ((0, 2),)),
    }


EPS = 1e-06

def gelu_tanh(value):
    return jax.nn.gelu(value, approximate=True)

def norm_rows(rows, gain):
    values = rows.astype(jnp.float32)
    width = rows.shape[1]
    mean = lax.optimization_barrier(jnp.sum(values, axis=1)) / width
    var = lax.optimization_barrier(jnp.sum(values * values, axis=1)) / width - mean * mean
    scaled = (values - mean[:, None]) * lax.rsqrt(var + EPS)[:, None] * gain.astype(jnp.float32)[None, :]
    return scaled.astype(jnp.bfloat16)

def reference(teacher_rows, teacher_gain, head_weight, student_slot, student_rows, student_gain, up_weight, down_weight):
    normed_t = norm_rows(teacher_rows, teacher_gain)
    target = jnp.dot(normed_t, head_weight, preferred_element_type=jnp.float32).astype(jnp.bfloat16)
    arrived = jnp.zeros_like(target).at[student_slot].set(target)
    normed_s = norm_rows(student_rows, student_gain)
    pre = jnp.dot(normed_s, up_weight, preferred_element_type=jnp.float32)
    act_value, pull = jax.vjp(gelu_tanh, pre)
    act = act_value.astype(jnp.bfloat16)
    output = jnp.dot(act, down_weight, preferred_element_type=jnp.float32)
    scale = lax.rsqrt(jnp.asarray(TOKENS, jnp.float32))
    diff = ((output - arrived.astype(jnp.float32)) * scale).astype(jnp.bfloat16)
    grad_down = jnp.dot(act.T, diff, preferred_element_type=jnp.float32)
    back = jnp.dot(diff, down_weight.T, preferred_element_type=jnp.float32)
    dpre = pull(back)[0].astype(jnp.bfloat16)
    grad_up = jnp.dot(normed_s.T, dpre, preferred_element_type=jnp.float32)
    return (grad_up, grad_down)
```

```python
import functools

import jax
import jax.numpy as jnp
from jax import lax
from jax.experimental import pallas as pl
from jax.experimental.pallas import tpu as pltpu
from jax.sharding import PartitionSpec as P

EPS = 1e-06
MESH = pl.DeviceIdType.MESH


def gelu_tanh(value):
    return jax.nn.gelu(value, approximate=True)


def scale_rows(values, mean, var, gain):
    scaled = (
        (values - mean[:, None]) * lax.rsqrt(var + EPS)[:, None] * gain.astype(jnp.float32)[None, :]
    )
    return scaled.astype(jnp.bfloat16)


def move_rows(values, slots):
    peers = lax.axis_size("batch")
    rows = slots.shape[0]
    capacity = 2 * rows // peers
    owner = slots // rows
    local = slots % rows
    onehot = (owner[:, None] == jnp.arange(peers, dtype=jnp.int32)[None, :]).astype(jnp.int32)
    rank = jnp.sum((jnp.cumsum(onehot, axis=0) - onehot) * onehot, axis=1)
    flat = owner * capacity + rank
    buffer = jnp.zeros((peers * capacity, values.shape[1]), values.dtype).at[flat].set(values)
    places = jnp.full((peers * capacity,), rows, jnp.int32).at[flat].set(local)
    got, where = (
        lax.all_to_all(
            buffer.reshape(peers, capacity, values.shape[1]),
            "batch",
            split_axis=0,
            concat_axis=0,
            tiled=True,
        ),
        lax.all_to_all(
            places.reshape(peers, capacity), "batch", split_axis=0, concat_axis=0, tiled=True
        ),
    )
    return (
        jnp.zeros_like(values)
        .at[where.reshape(-1)]
        .set(got.reshape(peers * capacity, values.shape[1]), mode="drop")
    )


def grads_kernel(
    length, norm_ref, dpre_ref, diff_ref, act_ref, up_ref, down_ref,
    left_t, y_out, y_in, z_out, z_in, y_send, y_recv, z_send, z_recv,
):
    me = lax.axis_index("batch")
    pos, side = me // 2, me % 2
    other = 1 - side
    half = pos // (length // 2)
    block = up_ref.shape[0]
    rights = (dpre_ref, act_ref)

    barrier = pltpu.get_barrier_semaphore()
    pl.semaphore_signal(barrier, inc=1, device_id={"batch": pos * 2 + other}, device_id_type=MESH)

    @pl.when(pos > 0)
    def _():
        pl.semaphore_signal(barrier, inc=1, device_id={"batch": me - 2}, device_id_type=MESH)

    @pl.when(pos < length - 1)
    def _():
        pl.semaphore_signal(barrier, inc=1, device_id={"batch": me + 2}, device_id_type=MESH)

    left_t[0] = norm_ref[...].T
    left_t[1] = diff_ref[...].T

    pl.semaphore_wait(barrier, 1 + (pos + length - 1) // length + 1 - (pos + 1) // length)

    def product(which, spot, at_side):
        start = pl.multiple_of((spot * 2 + at_side) * block, block)
        return jnp.dot(
            left_t[which, pl.ds(start, block), :], rights[which][...],
            preferred_element_type=jnp.float32,
        )

    def pair_copy(spot, which):
        return pltpu.make_async_remote_copy(
            src_ref=y_out.at[spot, which], dst_ref=y_in.at[spot, which],
            send_sem=y_send.at[spot, which], recv_sem=y_recv.at[spot, which],
            device_id={"batch": pos * 2 + other}, device_id_type=MESH,
        )

    def line_copy(way, step, which, target):
        return pltpu.make_async_remote_copy(
            src_ref=z_out.at[way, step, which], dst_ref=z_in.at[way, step, which],
            send_sem=z_send.at[way, step, which], recv_sem=z_recv.at[way, step, which],
            device_id={"batch": target}, device_id_type=MESH,
        )

    def moves():
        for step in range(length - 1):
            up_spot, down_spot = length - 1 - step, step
            yield step, half, (1 - half) * up_spot + half * down_spot, 1 - 2 * half
            yield step, 1 - half, half * up_spot + (1 - half) * down_spot, 2 * half - 1

    def start_pair(spot):
        for which in (1, 0):
            y_out[spot, which] = product(which, spot, other).astype(y_out.dtype)
            pair_copy(spot, which).start()

    for step, way, spot, sign in moves():
        @pl.when((spot - pos) * sign > 0)
        def _():
            start_pair(spot)

    start_pair(pos)

    for step, way, spot, sign in moves():
        has_before = jnp.logical_and(pos - sign >= 0, pos - sign <= length - 1)

        @pl.when((spot - pos) * sign > 0)
        def _():
            for which in (1, 0):
                mine = product(which, spot, side)
                pair_copy(spot, which).wait_recv()
                mine = mine + y_in[spot, which].astype(jnp.float32)

                @pl.when(has_before)
                def _():
                    line_copy(way, step, which, me).wait_recv()
                    total = mine + z_in[way, step, which].astype(jnp.float32)
                    z_out[way, step, which] = total.astype(z_out.dtype)

                @pl.when(jnp.logical_not(has_before))
                def _():
                    z_out[way, step, which] = mine.astype(z_out.dtype)

                line_copy(way, step, which, me + 2 * sign).start()

    outs = (up_ref, down_ref)
    for which in (1, 0):
        mine = product(which, pos, side)
        pair_copy(pos, which).wait_recv()
        outs[which][...] = mine + y_in[pos, which].astype(jnp.float32)

    for which in (1, 0):
        @pl.when(pos > 0)
        def _():
            step = length - 1 - pos
            line_copy(0, step, which, me).wait_recv()
            outs[which][...] += z_in[0, step, which].astype(jnp.float32)

        @pl.when(pos < length - 1)
        def _():
            line_copy(1, pos, which, me).wait_recv()
            outs[which][...] += z_in[1, pos, which].astype(jnp.float32)

    for spot in range(length):
        for which in (1, 0):
            pair_copy(spot, which).wait_send()
    for step, way, spot, sign in moves():
        @pl.when((spot - pos) * sign > 0)
        def _():
            for which in (1, 0):
                line_copy(way, step, which, me).wait_send()


def sum_grads(normed, dpre, diff, act):
    peers = lax.axis_size("batch")
    length = peers // 2
    rows, inner = normed.shape
    hidden = dpre.shape[1]
    block = inner // peers
    line_type = jnp.bfloat16 if length <= 4 else jnp.float32
    vmem = pl.BlockSpec(memory_space=pltpu.VMEM)
    result = jax.ShapeDtypeStruct((block, hidden), jnp.float32)
    line = (2, length - 1, 2)
    up, down_t = pl.pallas_call(
        functools.partial(grads_kernel, length),
        out_shape=(result, result),
        in_specs=[vmem] * 4,
        out_specs=(vmem, vmem),
        scratch_shapes=[
            pltpu.VMEM((2, inner, rows), jnp.bfloat16),
            pltpu.VMEM((length, 2, block, hidden), jnp.bfloat16),
            pltpu.VMEM((length, 2, block, hidden), jnp.bfloat16),
            pltpu.VMEM(line + (block, hidden), line_type),
            pltpu.VMEM(line + (block, hidden), line_type),
            pltpu.SemaphoreType.DMA((length, 2)),
            pltpu.SemaphoreType.DMA((length, 2)),
            pltpu.SemaphoreType.DMA(line),
            pltpu.SemaphoreType.DMA(line),
        ],
        compiler_params=pltpu.CompilerParams(
            collective_id=1, has_side_effects=True, vmem_limit_bytes=56 * 1024 * 1024
        ),
        cost_estimate=pl.CostEstimate(
            flops=4 * rows * inner * hidden, bytes_accessed=8 * rows * inner, transcendentals=0
        ),
        name="sum_grads",
    )(normed, dpre, diff, act)
    return up, down_t.T


def body(
    teacher_rows,
    teacher_gain,
    head_weight,
    student_slot,
    student_rows,
    student_gain,
    up_weight,
    down_weight,
):
    peers = lax.axis_size("batch")
    rows = teacher_rows.shape[0]
    teacher_vals = teacher_rows.astype(jnp.float32)
    width_t = teacher_rows.shape[1] * lax.axis_size("tensor")
    total, total_sq = lax.psum(
        (jnp.sum(teacher_vals, axis=1), jnp.sum(teacher_vals * teacher_vals, axis=1)), "tensor"
    )
    mean_t = total / width_t
    var_t = total_sq / width_t - mean_t * mean_t
    normed_t = scale_rows(teacher_vals, mean_t, var_t, teacher_gain)
    partial_value = jnp.dot(normed_t, head_weight, preferred_element_type=jnp.float32)
    target = lax.psum(partial_value, "tensor").astype(jnp.bfloat16)
    arrived = move_rows(target, student_slot)
    student_vals = student_rows.astype(jnp.float32)
    width_s = student_rows.shape[1]
    mean_s = jnp.sum(student_vals, axis=1) / width_s
    var_s = jnp.sum(student_vals * student_vals, axis=1) / width_s - mean_s * mean_s
    normed_s = scale_rows(student_vals, mean_s, var_s, student_gain)
    pre = jnp.dot(normed_s, up_weight, preferred_element_type=jnp.float32)
    act_value, pull = jax.vjp(gelu_tanh, pre)
    act = act_value.astype(jnp.bfloat16)
    out_part = jnp.dot(act, down_weight, preferred_element_type=jnp.float32)
    scale = lax.rsqrt(jnp.asarray(rows * peers, jnp.float32))
    out_full = lax.psum(out_part, "tensor")
    diff = ((out_full - arrived.astype(jnp.float32)) * scale).astype(jnp.bfloat16)
    back = jnp.einsum("td,hd->th", diff, down_weight, preferred_element_type=jnp.float32)
    dpre = pull(back)[0].astype(jnp.bfloat16)
    return sum_grads(normed_s, dpre, diff, act)


def solution(mesh):
    return jax.shard_map(
        body,
        mesh=mesh,
        in_specs=(
            P(("groups", "batch"), "tensor"),
            P("tensor"),
            P("tensor", None),
            P(("groups", "batch")),
            P(("groups", "batch"), None),
            P(),
            P(None, "tensor"),
            P("tensor", None),
        ),
        out_specs=(P(("groups", "batch"), "tensor"), P(("groups", "tensor"), "batch")),
        check_vma=False,
    )
```

```python
import functools

import jax
import jax.numpy as jnp
from jax import lax
from jax.experimental import pallas as pl
from jax.experimental.pallas import tpu as pltpu
from jax.sharding import PartitionSpec as P

EPS = 1e-06
MESH = pl.DeviceIdType.MESH


def step_kernel(
    length, cap, teacher_hbm, head_hbm, student_hbm, up_hbm, down_hbm, gain_t_ref, gain_s_ref,
    slot_row, slot_col, up_ref, down_ref,
    teacher, head, student, up, down, stat_out, stat_in, part, part_in, target,
    place_out, place_in, pack, got, flat_row, flat_col, norm, slope, act, out, out_in, arrived,
    diff, diff_in, dpre, left_t, y_out, y_in, z_out, z_in,
    load, core_send, core_recv, part_send, part_recv, place_send, place_recv, pack_send, pack_recv,
    y_send, y_recv, z_send, z_recv,
):
    me = lax.axis_index("batch")
    core = lax.axis_index("tensor")
    mate = 1 - core
    peers = 2 * length
    rows, wide = teacher.shape
    narrow = student.shape[1]
    cols = narrow // 2
    pos, side = me // 2, me % 2
    other = 1 - side
    half = pos // (length // 2)
    block = up_ref.shape[0]

    loads = [
        pltpu.make_async_copy(src, dst, load.at[i])
        for i, (src, dst) in enumerate(
            ((teacher_hbm, teacher), (head_hbm, head), (student_hbm, student), (up_hbm, up), (down_hbm, down))
        )
    ]
    for one in loads:
        one.start()

    barrier = pltpu.get_barrier_semaphore()
    pl.semaphore_signal(barrier, inc=1, device_id={"tensor": mate}, device_id_type=MESH)

    @pl.loop(1, peers)
    def _(i):
        pl.semaphore_signal(
            barrier, inc=1, device_id={"batch": (me + i) % peers}, device_id_type=MESH
        )

    def to_mate(index, src, dst):
        return pltpu.make_async_remote_copy(
            src_ref=src, dst_ref=dst, send_sem=core_send.at[index], recv_sem=core_recv.at[index],
            device_id={"tensor": mate}, device_id_type=MESH,
        )

    shift = rows.bit_length() - 1
    owner_row, owner_col = slot_row[...] >> shift, slot_col[...] >> shift
    same = owner_col == owner_row
    sub = lax.broadcasted_iota(jnp.int32, (rows, rows), 0)
    lane = lax.broadcasted_iota(jnp.int32, (rows, rows), 1)
    rank_row = jnp.sum(jnp.where(same & (sub < lane), 1, 0), axis=0, keepdims=True)
    rank_col = jnp.sum(jnp.where(same & (lane < sub), 1, 0), axis=1, keepdims=True)
    flat_row[...] = owner_row * cap + rank_row
    flat_col[...] = owner_col * cap + rank_col

    loads[0].wait()
    small = 32

    @pl.loop(0, rows // small)
    def _(i):
        at = pl.ds(pl.multiple_of(i * small, small), small)
        vals = teacher[at, :].astype(jnp.float32)
        total = jnp.sum(vals, axis=1, keepdims=True)
        squares = jnp.sum(vals * vals, axis=1, keepdims=True)
        spot = lax.broadcasted_iota(jnp.int32, (small, 128), 1)
        stat_out[at, :] = jnp.where(spot < 64, total, squares)

    pl.semaphore_wait(barrier, peers)
    swap_stat = to_mate(0, stat_out, stat_in)
    swap_stat.start()

    def place_copy(target_at, slot):
        return pltpu.make_async_remote_copy(
            src_ref=place_out.at[target_at], dst_ref=place_in.at[slot],
            send_sem=place_send.at[target_at], recv_sem=place_recv.at[slot],
            device_id={"batch": target_at}, device_id_type=MESH,
        )

    def places(target_at):
        spot = lax.broadcasted_iota(jnp.int32, (rows, cap), 1) + target_at * cap
        local = (slot_col[...] & (rows - 1)) + 1
        found = jnp.sum(jnp.where(flat_col[...] == spot, local, 0), axis=0, keepdims=True) - 1
        return jnp.broadcast_to(found, (8, cap))

    @pl.loop(1, peers)
    def _(i):
        target_at = (me + i) % peers
        place_out[target_at] = places(target_at)
        place_copy(target_at, me).start()

    place_in[me] = places(me)

    swap_stat.wait_recv()

    @pl.loop(0, rows // small)
    def _(i):
        at = pl.ds(pl.multiple_of(i * small, small), small)
        both = stat_out[at, :] + stat_in[at, :]
        mean = both[:, 0:1] / (2 * wide)
        var = both[:, 64:65] / (2 * wide) - mean * mean
        vals = teacher[at, :].astype(jnp.float32)
        scaled = (vals - mean) * lax.rsqrt(var + EPS) * gain_t_ref[...].astype(jnp.float32)
        teacher[at, :] = scaled.astype(jnp.bfloat16)

    loads[1].wait()
    large = rows // 2

    def part_copy(i):
        at = pl.ds(pl.multiple_of(i * large, large), large)
        return pltpu.make_async_remote_copy(
            src_ref=part.at[mate, at], dst_ref=part_in.at[at],
            send_sem=part_send.at[i], recv_sem=part_recv.at[i],
            device_id={"tensor": mate}, device_id_type=MESH,
        )

    @pl.loop(0, 2)
    def _(i):
        at = pl.ds(pl.multiple_of(i * large, large), large)
        value = jnp.dot(teacher[at, :], head[...], preferred_element_type=jnp.float32)
        part[0, at, :] = value[:, :cols]
        part[1, at, :] = value[:, cols:]
        part_copy(i).start()

    for i in range(2):
        part_copy(i).wait_recv()
        at = pl.ds(i * large, large)
        target[at, :] = (part[core, at, :] + part_in[at, :]).astype(jnp.bfloat16)

    def pack_copy(target_at, slot):
        return pltpu.make_async_remote_copy(
            src_ref=pack.at[target_at], dst_ref=got.at[slot],
            send_sem=pack_send.at[target_at], recv_sem=pack_recv.at[slot],
            device_id={"batch": target_at}, device_id_type=MESH,
        )

    def packed(target_at):
        spot = lax.broadcasted_iota(jnp.int32, (cap, rows), 0) + target_at * cap
        pick = jnp.where(flat_row[...] == spot, 1.0, 0.0).astype(jnp.bfloat16)
        return jnp.dot(pick, target[...], preferred_element_type=jnp.float32).astype(jnp.bfloat16)

    @pl.loop(1, peers)
    def _(i):
        target_at = (me + i) % peers
        pack[target_at] = packed(target_at)
        pack_copy(target_at, me).start()

    got[me] = packed(me)

    for one in loads[2:]:
        one.wait()
    middle = rows // 4
    root = 0.7978845608028654
    cube = 0.044715

    @pl.loop(0, rows // middle)
    def _(i):
        at = pl.ds(pl.multiple_of(i * middle, middle), middle)
        vals = student[at, :].astype(jnp.float32)
        mean = jnp.sum(vals, axis=1, keepdims=True) / narrow
        var = jnp.sum(vals * vals, axis=1, keepdims=True) / narrow - mean * mean
        scaled = (vals - mean) * lax.rsqrt(var + EPS) * gain_s_ref[...].astype(jnp.float32)
        norm[at, :] = scaled.astype(jnp.bfloat16)
        pre = jnp.dot(norm[at, :], up[...], preferred_element_type=jnp.float32)
        square = pre * pre
        bend = jnp.tanh(root * (pre + cube * (square * pre)))
        act[at, :] = (0.5 * pre * (1.0 + bend)).astype(jnp.bfloat16)
        slope[at, :] = 0.5 * (1.0 + bend) + 0.5 * pre * (1.0 - bend * bend) * (
            root * (1.0 + 3.0 * cube * square)
        )
        value = jnp.dot(act[at, :], down[...], preferred_element_type=jnp.float32)
        out[0, at, :] = value[:, :cols]
        out[1, at, :] = value[:, cols:]

    swap_out = to_mate(1, out.at[mate], out_in)
    swap_out.start()
    left_t[0] = norm[...].T
    swap_out.wait_recv()

    arrived[...] = jnp.zeros_like(arrived)

    def unpack(slot):
        spot = lax.broadcasted_iota(jnp.int32, (rows, cap), 0)
        put = jnp.where(place_in[slot, 0:1, :] == spot, 1.0, 0.0).astype(jnp.bfloat16)
        arrived[...] += jnp.dot(put, got[slot], preferred_element_type=jnp.float32)

    unpack(me)

    @pl.loop(1, peers)
    def _(i):
        source = (me + peers - i) % peers
        place_copy(source, source).wait_recv()
        pack_copy(source, source).wait_recv()
        unpack(source)

    scale = 1.0 / float(rows * peers) ** 0.5
    diff[...] = ((out[core] + out_in[...] - arrived[...]) * scale).astype(jnp.bfloat16)
    swap_diff = to_mate(2, diff, diff_in)
    swap_diff.start()
    left_t[1, pl.ds(pl.multiple_of(core * cols, cols), cols), :] = diff[...].T
    swap_diff.wait_recv()
    left_t[1, pl.ds(pl.multiple_of(mate * cols, cols), cols), :] = diff_in[...].T

    rights = (dpre, act)

    def product(which, spot, at_side):
        start = pl.multiple_of((spot * 2 + at_side) * block, block)
        return jnp.dot(
            left_t[which, pl.ds(start, block), :], rights[which][...],
            preferred_element_type=jnp.float32,
        )

    def pair_copy(spot, which):
        return pltpu.make_async_remote_copy(
            src_ref=y_out.at[spot, which], dst_ref=y_in.at[spot, which],
            send_sem=y_send.at[spot, which], recv_sem=y_recv.at[spot, which],
            device_id={"batch": pos * 2 + other}, device_id_type=MESH,
        )

    def line_copy(way, step, which, target_at):
        return pltpu.make_async_remote_copy(
            src_ref=z_out.at[way, step, which], dst_ref=z_in.at[way, step, which],
            send_sem=z_send.at[way, step, which], recv_sem=z_recv.at[way, step, which],
            device_id={"batch": target_at}, device_id_type=MESH,
        )

    def moves():
        for step in range(length - 1):
            up_spot, down_spot = length - 1 - step, step
            yield step, half, (1 - half) * up_spot + half * down_spot, 1 - 2 * half
            yield step, 1 - half, half * up_spot + (1 - half) * down_spot, 2 * half - 1

    def start_pairs(which):
        def start_pair(spot):
            y_out[spot, which] = product(which, spot, other).astype(y_out.dtype)
            pair_copy(spot, which).start()

        for step, way, spot, sign in moves():
            @pl.when((spot - pos) * sign > 0)
            def _():
                start_pair(spot)

        start_pair(pos)

    start_pairs(1)

    @pl.loop(0, rows // middle)
    def _(i):
        at = pl.ds(pl.multiple_of(i * middle, middle), middle)
        contract = (((1,), (1,)), ((), ()))

        def back_of(piece, which):
            lanes = pl.ds(pl.multiple_of(which * cols, cols), cols)
            return lax.dot_general(
                piece[at, :], down[:, lanes], contract, preferred_element_type=jnp.float32
            )

        back = back_of(diff, core) + back_of(diff_in, mate)
        dpre[at, :] = (back * slope[at, :]).astype(jnp.bfloat16)

    start_pairs(0)

    outs = (up_ref, down_ref)
    for which in (1, 0):
        for step, way, spot, sign in moves():
            has_before = jnp.logical_and(pos - sign >= 0, pos - sign <= length - 1)

            @pl.when((spot - pos) * sign > 0)
            def _():
                mine = product(which, spot, side)
                pair_copy(spot, which).wait_recv()
                mine = mine + y_in[spot, which].astype(jnp.float32)

                @pl.when(has_before)
                def _():
                    line_copy(way, step, which, me).wait_recv()
                    total = mine + z_in[way, step, which].astype(jnp.float32)
                    z_out[way, step, which] = total.astype(z_out.dtype)

                @pl.when(jnp.logical_not(has_before))
                def _():
                    z_out[way, step, which] = mine.astype(z_out.dtype)

                line_copy(way, step, which, me + 2 * sign).start()

    for which in (1, 0):
        mine = product(which, pos, side)
        pair_copy(pos, which).wait_recv()
        outs[which][...] = mine + y_in[pos, which].astype(jnp.float32)

    for which in (1, 0):
        @pl.when(pos > 0)
        def _():
            step = length - 1 - pos
            line_copy(0, step, which, me).wait_recv()
            outs[which][...] += z_in[0, step, which].astype(jnp.float32)

        @pl.when(pos < length - 1)
        def _():
            line_copy(1, pos, which, me).wait_recv()
            outs[which][...] += z_in[1, pos, which].astype(jnp.float32)

    swap_stat.wait_send()
    swap_out.wait_send()
    swap_diff.wait_send()
    for i in range(2):
        part_copy(i).wait_send()

    @pl.loop(1, peers)
    def _(i):
        target_at = (me + i) % peers
        place_copy(target_at, me).wait_send()
        pack_copy(target_at, me).wait_send()

    for which in (1, 0):
        for spot in range(length):
            pair_copy(spot, which).wait_send()
        for step, way, spot, sign in moves():
            @pl.when((spot - pos) * sign > 0)
            def _():
                line_copy(way, step, which, me).wait_send()


def body(
    teacher_rows,
    teacher_gain,
    head_weight,
    student_slot,
    student_rows,
    student_gain,
    up_weight,
    down_weight,
):
    peers = lax.axis_size("batch")
    length = peers // 2
    rows, wide = teacher_rows.shape
    narrow = student_rows.shape[1]
    hidden = up_weight.shape[1]
    cols = narrow // 2
    cap = 2 * rows // peers
    block = narrow // peers
    line_type = jnp.bfloat16 if length <= 4 else jnp.float32
    half, single = jnp.bfloat16, jnp.float32
    vmem = pl.BlockSpec(memory_space=pltpu.VMEM)
    far = pl.BlockSpec(memory_space=pl.ANY)
    result = jax.ShapeDtypeStruct((block, hidden), single)
    line = (2, length - 1, 2)
    dma = pltpu.SemaphoreType.DMA
    up, down_t = pl.pallas_call(
        functools.partial(step_kernel, length, cap),
        out_shape=(result, result),
        in_specs=[far] * 5 + [vmem] * 4,
        out_specs=(vmem, vmem),
        scratch_shapes=[
            pltpu.VMEM((rows, wide), half),
            pltpu.VMEM((wide, narrow), half),
            pltpu.VMEM((rows, narrow), half),
            pltpu.VMEM((narrow, hidden), half),
            pltpu.VMEM((hidden, narrow), half),
            pltpu.VMEM((rows, 128), single),
            pltpu.VMEM((rows, 128), single),
            pltpu.VMEM((2, rows, cols), single),
            pltpu.VMEM((rows, cols), single),
            pltpu.VMEM((rows, cols), half),
            pltpu.VMEM((peers, 8, cap), jnp.int32),
            pltpu.VMEM((peers, 8, cap), jnp.int32),
            pltpu.VMEM((peers, cap, cols), half),
            pltpu.VMEM((peers, cap, cols), half),
            pltpu.VMEM((1, rows), jnp.int32),
            pltpu.VMEM((rows, 1), jnp.int32),
            pltpu.VMEM((rows, narrow), half),
            pltpu.VMEM((rows, hidden), single),
            pltpu.VMEM((rows, hidden), half),
            pltpu.VMEM((2, rows, cols), single),
            pltpu.VMEM((rows, cols), single),
            pltpu.VMEM((rows, cols), single),
            pltpu.VMEM((rows, cols), half),
            pltpu.VMEM((rows, cols), half),
            pltpu.VMEM((rows, hidden), half),
            pltpu.VMEM((2, narrow, rows), half),
            pltpu.VMEM((length, 2, block, hidden), half),
            pltpu.VMEM((length, 2, block, hidden), half),
            pltpu.VMEM(line + (block, hidden), line_type),
            pltpu.VMEM(line + (block, hidden), line_type),
            dma((5,)),
            dma((3,)),
            dma((3,)),
            dma((2,)),
            dma((2,)),
            dma((peers,)),
            dma((peers,)),
            dma((peers,)),
            dma((peers,)),
            dma((length, 2)),
            dma((length, 2)),
            dma(line),
            dma(line),
        ],
        compiler_params=pltpu.CompilerParams(
            collective_id=1, has_side_effects=True, vmem_limit_bytes=60 * 1024 * 1024
        ),
        name="step",
    )(
        teacher_rows, head_weight, student_rows, up_weight, down_weight,
        teacher_gain.reshape(1, wide), student_gain.reshape(1, narrow),
        student_slot.reshape(1, rows), student_slot.reshape(rows, 1),
    )
    return up, down_t.T


def solution(mesh):
    return jax.shard_map(
        body,
        mesh=mesh,
        in_specs=(
            P(("groups", "batch"), "tensor"),
            P("tensor"),
            P("tensor", None),
            P(("groups", "batch")),
            P(("groups", "batch"), None),
            P(),
            P(None, "tensor"),
            P("tensor", None),
        ),
        out_specs=(P(("groups", "batch"), "tensor"), P(("groups", "tensor"), "batch")),
        check_vma=False,
    )
```

```python
import functools

import jax
import jax.numpy as jnp
from jax import lax
from jax.experimental import pallas as pl
from jax.experimental.pallas import tpu as pltpu
from jax.sharding import PartitionSpec as P

EPS = 1e-06
MESH = pl.DeviceIdType.MESH


def step_kernel(
    length, cap, teacher_hbm, head_hbm, student_hbm, up_hbm, down_hbm, gains_ref,
    slot_row, up_ref, down_ref,
    teacher, head, student, up, down, stat_out, stat_in, part, part_in, target,
    place_out, place_in, pack, got, slot_col, flat_row, flat_col, norm, slope, act, out, out_in, arrived,
    diff, diff_in, dpre, left_t, y_out, y_in, z_out, z_in,
    load, core_send, core_recv, part_send, part_recv, place_send, place_recv, pack_send, pack_recv,
    y_send, y_recv, z_send, z_recv,
):
    me = lax.axis_index("batch")
    core = lax.axis_index("tensor")
    mate = 1 - core
    peers = 2 * length
    rows, wide = teacher.shape
    narrow = student.shape[1]
    cols = narrow // 2
    chunk = cols // 2
    pos, side = me // 2, me % 2
    other = 1 - side
    half = pos // (length // 2)
    block = up_ref.shape[0]

    loads = [
        pltpu.make_async_copy(src, dst, load.at[i])
        for i, (src, dst) in enumerate(
            ((teacher_hbm, teacher), (head_hbm, head), (student_hbm, student), (up_hbm, up), (down_hbm, down))
        )
    ]
    for one in loads:
        one.start()

    barrier = pltpu.get_barrier_semaphore()
    pl.semaphore_signal(barrier, inc=1, device_id={"tensor": mate}, device_id_type=MESH)

    @pl.loop(1, peers)
    def _(i):
        pl.semaphore_signal(
            barrier, inc=1, device_id={"batch": (me + i) % peers}, device_id_type=MESH
        )

    def to_mate(index, src, dst):
        return pltpu.make_async_remote_copy(
            src_ref=src, dst_ref=dst, send_sem=core_send.at[index], recv_sem=core_recv.at[index],
            device_id={"tensor": mate}, device_id_type=MESH,
        )

    shift = rows.bit_length() - 1
    slot_col[...] = jnp.broadcast_to(slot_row[...], (128, rows)).T[:, 0:1]
    owner_row, owner_col = slot_row[...] >> shift, slot_col[...] >> shift
    same = owner_col == owner_row
    sub = lax.broadcasted_iota(jnp.int32, (rows, rows), 0)
    lane = lax.broadcasted_iota(jnp.int32, (rows, rows), 1)
    rank_row = jnp.sum(jnp.where(same & (sub < lane), 1, 0), axis=0, keepdims=True)
    rank_col = jnp.sum(jnp.where(same & (lane < sub), 1, 0), axis=1, keepdims=True)
    flat_row[...] = owner_row * cap + rank_row
    flat_col[...] = owner_col * cap + rank_col

    loads[0].wait()
    small = 32

    @pl.loop(0, rows // small)
    def _(i):
        at = pl.ds(pl.multiple_of(i * small, small), small)
        vals = teacher[at, :].astype(jnp.float32)
        total = jnp.sum(vals, axis=1, keepdims=True)
        squares = jnp.sum(vals * vals, axis=1, keepdims=True)
        spot = lax.broadcasted_iota(jnp.int32, (small, 128), 1)
        stat_out[at, :] = jnp.where(spot < 64, total, squares)

    pl.semaphore_wait(barrier, peers)
    swap_stat = to_mate(0, stat_out, stat_in)
    swap_stat.start()

    def place_copy(target_at, slot):
        return pltpu.make_async_remote_copy(
            src_ref=place_out.at[target_at], dst_ref=place_in.at[slot],
            send_sem=place_send.at[target_at], recv_sem=place_recv.at[slot],
            device_id={"batch": target_at}, device_id_type=MESH,
        )

    def places(target_at):
        spot = lax.broadcasted_iota(jnp.int32, (rows, cap), 1) + target_at * cap
        local = (slot_col[...] & (rows - 1)) + 1
        found = jnp.sum(jnp.where(flat_col[...] == spot, local, 0), axis=0, keepdims=True) - 1
        return jnp.broadcast_to(found, (8, cap))

    @pl.loop(1, peers)
    def _(i):
        target_at = (me + i) % peers
        place_out[target_at] = places(target_at)
        place_copy(target_at, me).start()

    place_in[me] = places(me)

    swap_stat.wait_recv()

    @pl.loop(0, rows // small)
    def _(i):
        at = pl.ds(pl.multiple_of(i * small, small), small)
        both = stat_out[at, :] + stat_in[at, :]
        mean = both[:, 0:1] / (2 * wide)
        var = both[:, 64:65] / (2 * wide) - mean * mean
        vals = teacher[at, :].astype(jnp.float32)
        scaled = (vals - mean) * lax.rsqrt(var + EPS) * gains_ref[:, :wide]
        teacher[at, :] = scaled.astype(jnp.bfloat16)

    loads[1].wait()

    def part_copy(c):
        return pltpu.make_async_remote_copy(
            src_ref=part.at[c], dst_ref=part_in.at[c],
            send_sem=part_send.at[c], recv_sem=part_recv.at[c],
            device_id={"tensor": mate}, device_id_type=MESH,
        )

    def head_part(whose, c):
        lanes = pl.ds(pl.multiple_of(whose * cols + c * chunk, chunk), chunk)
        return jnp.dot(teacher[...], head[:, lanes], preferred_element_type=jnp.float32)

    def pack_copy(c, target_at, slot):
        return pltpu.make_async_remote_copy(
            src_ref=pack.at[c, target_at], dst_ref=got.at[c, slot],
            send_sem=pack_send.at[c, target_at], recv_sem=pack_recv.at[c, slot],
            device_id={"batch": target_at}, device_id_type=MESH,
        )

    def packed(c, target_at):
        spot = lax.broadcasted_iota(jnp.int32, (cap, rows), 0) + target_at * cap
        pick = jnp.where(flat_row[...] == spot, 1.0, 0.0).astype(jnp.bfloat16)
        return jnp.dot(pick, target[c], preferred_element_type=jnp.float32).astype(jnp.bfloat16)

    for c in range(2):
        part[c] = head_part(mate, c)
        part_copy(c).start()
        mine = head_part(core, c)
        part_copy(c).wait_recv()
        target[c] = (mine + part_in[c]).astype(jnp.bfloat16)

        @pl.loop(1, peers)
        def _(i):
            target_at = (me + i) % peers
            pack[c, target_at] = packed(c, target_at)
            pack_copy(c, target_at, me).start()

        got[c, me] = packed(c, me)

    for one in loads[2:]:
        one.wait()
    middle = rows // 4
    root = 0.7978845608028654
    cube = 0.044715

    @pl.loop(0, rows // middle)
    def _(i):
        at = pl.ds(pl.multiple_of(i * middle, middle), middle)
        vals = student[at, :].astype(jnp.float32)
        mean = jnp.sum(vals, axis=1, keepdims=True) / narrow
        var = jnp.sum(vals * vals, axis=1, keepdims=True) / narrow - mean * mean
        scaled = (vals - mean) * lax.rsqrt(var + EPS) * gains_ref[:, wide:]
        norm[at, :] = scaled.astype(jnp.bfloat16)
        pre = jnp.dot(norm[at, :], up[...], preferred_element_type=jnp.float32)
        square = pre * pre
        bend = jnp.tanh(root * (pre + cube * (square * pre)))
        act[at, :] = (0.5 * pre * (1.0 + bend)).astype(jnp.bfloat16)
        slope[at, :] = 0.5 * (1.0 + bend) + 0.5 * pre * (1.0 - bend * bend) * (
            root * (1.0 + 3.0 * cube * square)
        )
        value = jnp.dot(act[at, :], down[...], preferred_element_type=jnp.float32)
        out[0, at, :] = value[:, :cols]
        out[1, at, :] = value[:, cols:]

    swap_out = to_mate(1, out.at[mate], out_in)
    swap_out.start()
    left_t[0] = norm[...].T
    swap_out.wait_recv()

    scale = 1.0 / float(rows * peers) ** 0.5

    def put_of(slot):
        spot = lax.broadcasted_iota(jnp.int32, (rows, cap), 0)
        return jnp.where(place_in[slot, 0:1, :] == spot, 1.0, 0.0).astype(jnp.bfloat16)

    def diff_copy(c):
        return to_mate(2 + c, diff.at[c], diff_in.at[c])

    def turn(c, whose, piece):
        at = pl.ds(pl.multiple_of(whose * cols + c * chunk, chunk), chunk)
        left_t[1, at, :] = piece[c].T

    for c in range(2):
        arrived[...] = jnp.dot(put_of(me), got[c, me], preferred_element_type=jnp.float32)

        @pl.loop(1, peers)
        def _(i):
            source = (me + peers - i) % peers
            if c == 0:
                place_copy(source, source).wait_recv()
            pack_copy(c, source, source).wait_recv()
            arrived[...] += jnp.dot(
                put_of(source), got[c, source], preferred_element_type=jnp.float32
            )

        lanes = slice(c * chunk, (c + 1) * chunk)
        full = out[core, :, lanes] + out_in[:, lanes]
        diff[c] = ((full - arrived[...]) * scale).astype(jnp.bfloat16)
        diff_copy(c).start()
        turn(c, core, diff)

    for c in range(2):
        diff_copy(c).wait_recv()
        turn(c, mate, diff_in)

    rights = (dpre, act)

    def product(which, spot, at_side):
        start = pl.multiple_of((spot * 2 + at_side) * block, block)
        return jnp.dot(
            left_t[which, pl.ds(start, block), :], rights[which][...],
            preferred_element_type=jnp.float32,
        )

    def pair_copy(spot, which):
        return pltpu.make_async_remote_copy(
            src_ref=y_out.at[spot, which], dst_ref=y_in.at[spot, which],
            send_sem=y_send.at[spot, which], recv_sem=y_recv.at[spot, which],
            device_id={"batch": pos * 2 + other}, device_id_type=MESH,
        )

    def line_copy(way, step, which, target_at):
        return pltpu.make_async_remote_copy(
            src_ref=z_out.at[way, step, which], dst_ref=z_in.at[way, step, which],
            send_sem=z_send.at[way, step, which], recv_sem=z_recv.at[way, step, which],
            device_id={"batch": target_at}, device_id_type=MESH,
        )

    def moves():
        for step in range(length - 1):
            up_spot, down_spot = length - 1 - step, step
            yield step, half, (1 - half) * up_spot + half * down_spot, 1 - 2 * half
            yield step, 1 - half, half * up_spot + (1 - half) * down_spot, 2 * half - 1

    def start_pairs(which):
        def start_pair(spot):
            y_out[spot, which] = product(which, spot, other).astype(y_out.dtype)
            pair_copy(spot, which).start()

        for step, way, spot, sign in moves():
            @pl.when((spot - pos) * sign > 0)
            def _():
                start_pair(spot)

        start_pair(pos)

    start_pairs(1)

    @pl.loop(0, rows // middle)
    def _(i):
        at = pl.ds(pl.multiple_of(i * middle, middle), middle)
        contract = (((1,), (1,)), ((), ()))

        def back_of(piece, whose, c):
            lanes = pl.ds(pl.multiple_of(whose * cols + c * chunk, chunk), chunk)
            return lax.dot_general(
                piece[c, at, :], down[:, lanes], contract, preferred_element_type=jnp.float32
            )

        back = back_of(diff, core, 0) + back_of(diff, core, 1)
        back = back + back_of(diff_in, mate, 0) + back_of(diff_in, mate, 1)
        dpre[at, :] = (back * slope[at, :]).astype(jnp.bfloat16)

    start_pairs(0)

    outs = (up_ref, down_ref)
    for which in (1, 0):
        for step, way, spot, sign in moves():
            has_before = jnp.logical_and(pos - sign >= 0, pos - sign <= length - 1)

            @pl.when((spot - pos) * sign > 0)
            def _():
                mine = product(which, spot, side)
                pair_copy(spot, which).wait_recv()
                mine = mine + y_in[spot, which].astype(jnp.float32)

                @pl.when(has_before)
                def _():
                    line_copy(way, step, which, me).wait_recv()
                    total = mine + z_in[way, step, which].astype(jnp.float32)
                    z_out[way, step, which] = total.astype(z_out.dtype)

                @pl.when(jnp.logical_not(has_before))
                def _():
                    z_out[way, step, which] = mine.astype(z_out.dtype)

                line_copy(way, step, which, me + 2 * sign).start()

    for which in (1, 0):
        mine = product(which, pos, side)
        pair_copy(pos, which).wait_recv()
        outs[which][...] = mine + y_in[pos, which].astype(jnp.float32)

    for which in (1, 0):
        @pl.when(pos > 0)
        def _():
            step = length - 1 - pos
            line_copy(0, step, which, me).wait_recv()
            outs[which][...] += z_in[0, step, which].astype(jnp.float32)

        @pl.when(pos < length - 1)
        def _():
            line_copy(1, pos, which, me).wait_recv()
            outs[which][...] += z_in[1, pos, which].astype(jnp.float32)

    swap_stat.wait_send()
    swap_out.wait_send()
    for c in range(2):
        part_copy(c).wait_send()
        diff_copy(c).wait_send()

    @pl.loop(1, peers)
    def _(i):
        target_at = (me + i) % peers
        place_copy(target_at, me).wait_send()
        for c in range(2):
            pack_copy(c, target_at, me).wait_send()

    for which in (1, 0):
        for spot in range(length):
            pair_copy(spot, which).wait_send()
        for step, way, spot, sign in moves():
            @pl.when((spot - pos) * sign > 0)
            def _():
                line_copy(way, step, which, me).wait_send()


def place_kernel(up_ref, down_ref, up_out, down_out):
    up_out[...] = up_ref[...]
    down_out[...] = down_ref[...].T


def body(
    teacher_rows,
    teacher_gain,
    head_weight,
    student_slot,
    student_rows,
    student_gain,
    up_weight,
    down_weight,
):
    peers = lax.axis_size("batch")
    length = peers // 2
    rows, wide = teacher_rows.shape
    narrow = student_rows.shape[1]
    hidden = up_weight.shape[1]
    cols = narrow // 2
    cap = 2 * rows // peers
    block = narrow // peers
    line_type = jnp.bfloat16 if length <= 4 else jnp.float32
    half, single = jnp.bfloat16, jnp.float32
    vmem = pl.BlockSpec(memory_space=pltpu.VMEM)
    far = pl.BlockSpec(memory_space=pl.ANY)
    result = jax.ShapeDtypeStruct((block, hidden), single)
    line = (2, length - 1, 2)
    dma = pltpu.SemaphoreType.DMA
    up, down_t = pl.pallas_call(
        functools.partial(step_kernel, length, cap),
        out_shape=(result, result),
        in_specs=[far] * 5 + [vmem] * 2,
        out_specs=(vmem, vmem),
        scratch_shapes=[
            pltpu.VMEM((rows, wide), half),
            pltpu.VMEM((wide, narrow), half),
            pltpu.VMEM((rows, narrow), half),
            pltpu.VMEM((narrow, hidden), half),
            pltpu.VMEM((hidden, narrow), half),
            pltpu.VMEM((rows, 128), single),
            pltpu.VMEM((rows, 128), single),
            pltpu.VMEM((2, rows, cols // 2), single),
            pltpu.VMEM((2, rows, cols // 2), single),
            pltpu.VMEM((2, rows, cols // 2), half),
            pltpu.VMEM((peers, 8, cap), jnp.int32),
            pltpu.VMEM((peers, 8, cap), jnp.int32),
            pltpu.VMEM((2, peers, cap, cols // 2), half),
            pltpu.VMEM((2, peers, cap, cols // 2), half),
            pltpu.VMEM((rows, 1), jnp.int32),
            pltpu.VMEM((1, rows), jnp.int32),
            pltpu.VMEM((rows, 1), jnp.int32),
            pltpu.VMEM((rows, narrow), half),
            pltpu.VMEM((rows, hidden), single),
            pltpu.VMEM((rows, hidden), half),
            pltpu.VMEM((2, rows, cols), single),
            pltpu.VMEM((rows, cols), single),
            pltpu.VMEM((rows, cols // 2), single),
            pltpu.VMEM((2, rows, cols // 2), half),
            pltpu.VMEM((2, rows, cols // 2), half),
            pltpu.VMEM((rows, hidden), half),
            pltpu.VMEM((2, narrow, rows), half),
            pltpu.VMEM((length, 2, block, hidden), half),
            pltpu.VMEM((length, 2, block, hidden), half),
            pltpu.VMEM(line + (block, hidden), line_type),
            pltpu.VMEM(line + (block, hidden), line_type),
            dma((5,)),
            dma((4,)),
            dma((4,)),
            dma((2,)),
            dma((2,)),
            dma((peers,)),
            dma((peers,)),
            dma((2, peers)),
            dma((2, peers)),
            dma((length, 2)),
            dma((length, 2)),
            dma(line),
            dma(line),
        ],
        compiler_params=pltpu.CompilerParams(
            collective_id=1, has_side_effects=True, vmem_limit_bytes=60 * 1024 * 1024
        ),
        name="step",
    )(
        teacher_rows, head_weight, student_rows, up_weight, down_weight,
        jnp.concatenate([teacher_gain, student_gain]).astype(single).reshape(1, wide + narrow),
        student_slot.reshape(1, rows),
    )
    return pl.pallas_call(
        place_kernel,
        out_shape=(result, jax.ShapeDtypeStruct((hidden, block), single)),
        in_specs=[vmem] * 2,
        out_specs=(vmem, vmem),
        name="place",
    )(up, down_t)


def solution(mesh):
    return jax.shard_map(
        body,
        mesh=mesh,
        in_specs=(
            P(("groups", "batch"), "tensor"),
            P("tensor"),
            P("tensor", None),
            P(("groups", "batch")),
            P(("groups", "batch"), None),
            P(),
            P(None, "tensor"),
            P("tensor", None),
        ),
        out_specs=(P(("groups", "batch"), "tensor"), P(("groups", "tensor"), "batch")),
        check_vma=False,
    )
```

```python
import functools

import jax
import jax.numpy as jnp
from jax import lax
from jax.experimental import pallas as pl
from jax.experimental.pallas import tpu as pltpu
from jax.sharding import PartitionSpec as P

EPS = 1e-06
MESH = pl.DeviceIdType.MESH


def step_kernel(
    length, cap, teacher_hbm, head_hbm, student_hbm, up_hbm, down_hbm, gains_ref,
    slot_row, up_ref, down_ref,
    teacher, head, student, up, down, stat_out, stat_in, part, part_in, target,
    place_out, place_in, pack, got, slot_col, flat_row, flat_col, norm, slope, act, out, out_in, arrived,
    diff, diff_in, dpre, left_t, y_out, y_in, z_out, z_in,
    load, core_send, core_recv, part_send, part_recv, place_send, place_recv, pack_send, pack_recv,
    y_send, y_recv, z_send, z_recv,
):
    me = lax.axis_index("batch")
    core = lax.axis_index("tensor")
    mate = 1 - core
    peers = 2 * length
    rows, wide = teacher.shape
    narrow = student.shape[1]
    cols = narrow // 2
    chunk = cols // 2
    pos, side = me // 2, me % 2
    other = 1 - side
    half = pos // (length // 2)
    block = up_ref.shape[0]

    loads = [
        pltpu.make_async_copy(src, dst, load.at[i])
        for i, (src, dst) in enumerate(
            ((teacher_hbm, teacher), (head_hbm, head), (student_hbm, student), (up_hbm, up), (down_hbm, down))
        )
    ]
    for one in loads:
        one.start()

    barrier = pltpu.get_barrier_semaphore()
    pl.semaphore_signal(barrier, inc=1, device_id={"tensor": mate}, device_id_type=MESH)

    @pl.loop(1, peers)
    def _(i):
        pl.semaphore_signal(
            barrier, inc=1, device_id={"batch": (me + i) % peers}, device_id_type=MESH
        )

    def to_mate(index, src, dst):
        return pltpu.make_async_remote_copy(
            src_ref=src, dst_ref=dst, send_sem=core_send.at[index], recv_sem=core_recv.at[index],
            device_id={"tensor": mate}, device_id_type=MESH,
        )

    shift = rows.bit_length() - 1
    slot_col[...] = jnp.broadcast_to(slot_row[...], (128, rows)).T[:, 0:1]
    owner_row, owner_col = slot_row[...] >> shift, slot_col[...] >> shift
    same = owner_col == owner_row
    sub = lax.broadcasted_iota(jnp.int32, (rows, rows), 0)
    lane = lax.broadcasted_iota(jnp.int32, (rows, rows), 1)
    rank_row = jnp.sum(jnp.where(same & (sub < lane), 1, 0), axis=0, keepdims=True)
    rank_col = jnp.sum(jnp.where(same & (lane < sub), 1, 0), axis=1, keepdims=True)
    flat_row[...] = owner_row * cap + rank_row
    flat_col[...] = owner_col * cap + rank_col

    loads[0].wait()
    small = 32

    @pl.loop(0, rows // small, unroll=4)
    def _(i):
        at = pl.ds(pl.multiple_of(i * small, small), small)
        vals = teacher[at, :].astype(jnp.float32)
        total = jnp.sum(vals, axis=1, keepdims=True)
        squares = jnp.sum(vals * vals, axis=1, keepdims=True)
        spot = lax.broadcasted_iota(jnp.int32, (small, 128), 1)
        stat_out[at, :] = jnp.where(spot < 64, total, squares)

    pl.semaphore_wait(barrier, peers)
    swap_stat = to_mate(0, stat_out, stat_in)
    swap_stat.start()

    def place_copy(target_at, slot):
        return pltpu.make_async_remote_copy(
            src_ref=place_out.at[target_at], dst_ref=place_in.at[slot],
            send_sem=place_send.at[target_at], recv_sem=place_recv.at[slot],
            device_id={"batch": target_at}, device_id_type=MESH,
        )

    def places(target_at):
        spot = lax.broadcasted_iota(jnp.int32, (rows, cap), 1) + target_at * cap
        local = (slot_col[...] & (rows - 1)) + 1
        found = jnp.sum(jnp.where(flat_col[...] == spot, local, 0), axis=0, keepdims=True) - 1
        return jnp.broadcast_to(found, (8, cap))

    @pl.loop(1, peers)
    def _(i):
        target_at = (me + i) % peers
        place_out[target_at] = places(target_at)
        place_copy(target_at, me).start()

    place_in[me] = places(me)

    swap_stat.wait_recv()

    @pl.loop(0, rows // small, unroll=4)
    def _(i):
        at = pl.ds(pl.multiple_of(i * small, small), small)
        both = stat_out[at, :] + stat_in[at, :]
        mean = both[:, 0:1] / (2 * wide)
        var = both[:, 64:65] / (2 * wide) - mean * mean
        vals = teacher[at, :].astype(jnp.float32)
        scaled = (vals - mean) * lax.rsqrt(var + EPS) * gains_ref[:, :wide]
        teacher[at, :] = scaled.astype(jnp.bfloat16)

    loads[1].wait()

    def part_copy(c):
        return pltpu.make_async_remote_copy(
            src_ref=part.at[c], dst_ref=part_in.at[c],
            send_sem=part_send.at[c], recv_sem=part_recv.at[c],
            device_id={"tensor": mate}, device_id_type=MESH,
        )

    def head_part(whose, c):
        lanes = pl.ds(pl.multiple_of(whose * cols + c * chunk, chunk), chunk)
        return jnp.dot(teacher[...], head[:, lanes], preferred_element_type=jnp.float32)

    def pack_copy(c, target_at, slot):
        return pltpu.make_async_remote_copy(
            src_ref=pack.at[c, target_at], dst_ref=got.at[c, slot],
            send_sem=pack_send.at[c, target_at], recv_sem=pack_recv.at[c, slot],
            device_id={"batch": target_at}, device_id_type=MESH,
        )

    def packed(c, target_at):
        spot = lax.broadcasted_iota(jnp.int32, (cap, rows), 0) + target_at * cap
        pick = jnp.where(flat_row[...] == spot, 1.0, 0.0).astype(jnp.bfloat16)
        return jnp.dot(pick, target[c], preferred_element_type=jnp.float32).astype(jnp.bfloat16)

    for c in range(2):
        part[c] = head_part(mate, c)
        part_copy(c).start()
        mine = head_part(core, c)
        part_copy(c).wait_recv()
        target[c] = (mine + part_in[c]).astype(jnp.bfloat16)

        @pl.loop(1, peers)
        def _(i):
            target_at = (me + i) % peers
            pack[c, target_at] = packed(c, target_at)
            pack_copy(c, target_at, me).start()

        got[c, me] = packed(c, me)

    for one in loads[2:]:
        one.wait()
    middle = rows // 4
    root = 0.7978845608028654
    cube = 0.044715

    @pl.loop(0, rows // middle)
    def _(i):
        at = pl.ds(pl.multiple_of(i * middle, middle), middle)
        vals = student[at, :].astype(jnp.float32)
        mean = jnp.sum(vals, axis=1, keepdims=True) / narrow
        var = jnp.sum(vals * vals, axis=1, keepdims=True) / narrow - mean * mean
        scaled = (vals - mean) * lax.rsqrt(var + EPS) * gains_ref[:, wide:]
        norm[at, :] = scaled.astype(jnp.bfloat16)
        pre = jnp.dot(norm[at, :], up[...], preferred_element_type=jnp.float32)
        square = pre * pre
        bend = jnp.tanh(root * (pre + cube * (square * pre)))
        act[at, :] = (0.5 * pre * (1.0 + bend)).astype(jnp.bfloat16)
        slope[at, :] = 0.5 * (1.0 + bend) + 0.5 * pre * (1.0 - bend * bend) * (
            root * (1.0 + 3.0 * cube * square)
        )
        value = jnp.dot(act[at, :], down[...], preferred_element_type=jnp.float32)
        out[0, at, :] = value[:, :cols]
        out[1, at, :] = value[:, cols:]

    swap_out = to_mate(1, out.at[mate], out_in)
    swap_out.start()
    left_t[0] = norm[...].T
    swap_out.wait_recv()

    scale = 1.0 / float(rows * peers) ** 0.5

    def put_of(slot):
        spot = lax.broadcasted_iota(jnp.int32, (rows, cap), 0)
        return jnp.where(place_in[slot, 0:1, :] == spot, 1.0, 0.0).astype(jnp.bfloat16)

    def diff_copy(c):
        return to_mate(2 + c, diff.at[c], diff_in.at[c])

    def turn(c, whose, piece):
        at = pl.ds(pl.multiple_of(whose * cols + c * chunk, chunk), chunk)
        left_t[1, at, :] = piece[c].T

    for c in range(2):
        arrived[...] = jnp.dot(put_of(me), got[c, me], preferred_element_type=jnp.float32)

        @pl.loop(1, peers)
        def _(i):
            source = (me + peers - i) % peers
            if c == 0:
                place_copy(source, source).wait_recv()
            pack_copy(c, source, source).wait_recv()
            arrived[...] += jnp.dot(
                put_of(source), got[c, source], preferred_element_type=jnp.float32
            )

        lanes = slice(c * chunk, (c + 1) * chunk)
        full = out[core, :, lanes] + out_in[:, lanes]
        diff[c] = ((full - arrived[...]) * scale).astype(jnp.bfloat16)
        diff_copy(c).start()
        turn(c, core, diff)

    for c in range(2):
        diff_copy(c).wait_recv()
        turn(c, mate, diff_in)

    rights = (dpre, act)

    def product(which, spot, at_side):
        start = pl.multiple_of((spot * 2 + at_side) * block, block)
        return jnp.dot(
            left_t[which, pl.ds(start, block), :], rights[which][...],
            preferred_element_type=jnp.float32,
        )

    def pair_copy(spot, which):
        return pltpu.make_async_remote_copy(
            src_ref=y_out.at[spot, which], dst_ref=y_in.at[spot, which],
            send_sem=y_send.at[spot, which], recv_sem=y_recv.at[spot, which],
            device_id={"batch": pos * 2 + other}, device_id_type=MESH,
        )

    def line_copy(way, step, which, target_at):
        return pltpu.make_async_remote_copy(
            src_ref=z_out.at[way, step, which], dst_ref=z_in.at[way, step, which],
            send_sem=z_send.at[way, step, which], recv_sem=z_recv.at[way, step, which],
            device_id={"batch": target_at}, device_id_type=MESH,
        )

    def moves():
        for step in range(length - 1):
            up_spot, down_spot = length - 1 - step, step
            yield step, half, (1 - half) * up_spot + half * down_spot, 1 - 2 * half
            yield step, 1 - half, half * up_spot + (1 - half) * down_spot, 2 * half - 1

    def start_pairs(which):
        def start_pair(spot):
            y_out[spot, which] = product(which, spot, other).astype(y_out.dtype)
            pair_copy(spot, which).start()

        for step, way, spot, sign in moves():
            @pl.when((spot - pos) * sign > 0)
            def _():
                start_pair(spot)

        start_pair(pos)

    start_pairs(1)

    @pl.loop(0, rows // middle)
    def _(i):
        at = pl.ds(pl.multiple_of(i * middle, middle), middle)
        contract = (((1,), (1,)), ((), ()))

        def back_of(piece, whose, c):
            lanes = pl.ds(pl.multiple_of(whose * cols + c * chunk, chunk), chunk)
            return lax.dot_general(
                piece[c, at, :], down[:, lanes], contract, preferred_element_type=jnp.float32
            )

        back = back_of(diff, core, 0) + back_of(diff, core, 1)
        back = back + back_of(diff_in, mate, 0) + back_of(diff_in, mate, 1)
        dpre[at, :] = (back * slope[at, :]).astype(jnp.bfloat16)

    start_pairs(0)

    outs = (up_ref, down_ref)
    for which in (1, 0):
        for step, way, spot, sign in moves():
            has_before = jnp.logical_and(pos - sign >= 0, pos - sign <= length - 1)

            @pl.when((spot - pos) * sign > 0)
            def _():
                mine = product(which, spot, side)
                pair_copy(spot, which).wait_recv()
                mine = mine + y_in[spot, which].astype(jnp.float32)

                @pl.when(has_before)
                def _():
                    line_copy(way, step, which, me).wait_recv()
                    total = mine + z_in[way, step, which].astype(jnp.float32)
                    z_out[way, step, which] = total.astype(z_out.dtype)

                @pl.when(jnp.logical_not(has_before))
                def _():
                    z_out[way, step, which] = mine.astype(z_out.dtype)

                line_copy(way, step, which, me + 2 * sign).start()

    for which in (1, 0):
        mine = product(which, pos, side)
        pair_copy(pos, which).wait_recv()
        outs[which][...] = mine + y_in[pos, which].astype(jnp.float32)

    for which in (1, 0):
        @pl.when(pos > 0)
        def _():
            step = length - 1 - pos
            line_copy(0, step, which, me).wait_recv()
            outs[which][...] += z_in[0, step, which].astype(jnp.float32)

        @pl.when(pos < length - 1)
        def _():
            line_copy(1, pos, which, me).wait_recv()
            outs[which][...] += z_in[1, pos, which].astype(jnp.float32)

    swap_stat.wait_send()
    swap_out.wait_send()
    for c in range(2):
        part_copy(c).wait_send()
        diff_copy(c).wait_send()

    @pl.loop(1, peers)
    def _(i):
        target_at = (me + i) % peers
        place_copy(target_at, me).wait_send()
        for c in range(2):
            pack_copy(c, target_at, me).wait_send()

    for which in (1, 0):
        for spot in range(length):
            pair_copy(spot, which).wait_send()
        for step, way, spot, sign in moves():
            @pl.when((spot - pos) * sign > 0)
            def _():
                line_copy(way, step, which, me).wait_send()


def place_kernel(up_ref, down_ref, up_out, down_out):
    up_out[...] = up_ref[...]
    down_out[...] = down_ref[...].T


def body(
    teacher_rows,
    teacher_gain,
    head_weight,
    student_slot,
    student_rows,
    student_gain,
    up_weight,
    down_weight,
):
    peers = lax.axis_size("batch")
    length = peers // 2
    rows, wide = teacher_rows.shape
    narrow = student_rows.shape[1]
    hidden = up_weight.shape[1]
    cols = narrow // 2
    cap = 2 * rows // peers
    block = narrow // peers
    line_type = jnp.bfloat16 if length <= 4 else jnp.float32
    half, single = jnp.bfloat16, jnp.float32
    vmem = pl.BlockSpec(memory_space=pltpu.VMEM)
    far = pl.BlockSpec(memory_space=pl.ANY)
    result = jax.ShapeDtypeStruct((block, hidden), single)
    line = (2, length - 1, 2)
    dma = pltpu.SemaphoreType.DMA
    up, down_t = pl.pallas_call(
        functools.partial(step_kernel, length, cap),
        out_shape=(result, result),
        in_specs=[far] * 5 + [vmem] * 2,
        out_specs=(vmem, vmem),
        scratch_shapes=[
            pltpu.VMEM((rows, wide), half),
            pltpu.VMEM((wide, narrow), half),
            pltpu.VMEM((rows, narrow), half),
            pltpu.VMEM((narrow, hidden), half),
            pltpu.VMEM((hidden, narrow), half),
            pltpu.VMEM((rows, 128), single),
            pltpu.VMEM((rows, 128), single),
            pltpu.VMEM((2, rows, cols // 2), single),
            pltpu.VMEM((2, rows, cols // 2), single),
            pltpu.VMEM((2, rows, cols // 2), half),
            pltpu.VMEM((peers, 8, cap), jnp.int32),
            pltpu.VMEM((peers, 8, cap), jnp.int32),
            pltpu.VMEM((2, peers, cap, cols // 2), half),
            pltpu.VMEM((2, peers, cap, cols // 2), half),
            pltpu.VMEM((rows, 1), jnp.int32),
            pltpu.VMEM((1, rows), jnp.int32),
            pltpu.VMEM((rows, 1), jnp.int32),
            pltpu.VMEM((rows, narrow), half),
            pltpu.VMEM((rows, hidden), single),
            pltpu.VMEM((rows, hidden), half),
            pltpu.VMEM((2, rows, cols), single),
            pltpu.VMEM((rows, cols), single),
            pltpu.VMEM((rows, cols // 2), single),
            pltpu.VMEM((2, rows, cols // 2), half),
            pltpu.VMEM((2, rows, cols // 2), half),
            pltpu.VMEM((rows, hidden), half),
            pltpu.VMEM((2, narrow, rows), half),
            pltpu.VMEM((length, 2, block, hidden), half),
            pltpu.VMEM((length, 2, block, hidden), half),
            pltpu.VMEM(line + (block, hidden), line_type),
            pltpu.VMEM(line + (block, hidden), line_type),
            dma((5,)),
            dma((4,)),
            dma((4,)),
            dma((2,)),
            dma((2,)),
            dma((peers,)),
            dma((peers,)),
            dma((2, peers)),
            dma((2, peers)),
            dma((length, 2)),
            dma((length, 2)),
            dma(line),
            dma(line),
        ],
        compiler_params=pltpu.CompilerParams(
            collective_id=1, has_side_effects=True, vmem_limit_bytes=60 * 1024 * 1024
        ),
        name="step",
    )(
        teacher_rows, head_weight, student_rows, up_weight, down_weight,
        jnp.concatenate([teacher_gain, student_gain]).astype(single).reshape(1, wide + narrow),
        student_slot.reshape(1, rows),
    )
    return pl.pallas_call(
        place_kernel,
        out_shape=(result, jax.ShapeDtypeStruct((hidden, block), single)),
        in_specs=[vmem] * 2,
        out_specs=(vmem, vmem),
        name="place",
    )(up, down_t)


def solution(mesh):
    return jax.shard_map(
        body,
        mesh=mesh,
        in_specs=(
            P(("groups", "batch"), "tensor"),
            P("tensor"),
            P("tensor", None),
            P(("groups", "batch")),
            P(("groups", "batch"), None),
            P(),
            P(None, "tensor"),
            P("tensor", None),
        ),
        out_specs=(P(("groups", "batch"), "tensor"), P(("groups", "tensor"), "batch")),
        check_vma=False,
    )
```
